32 devices in a mesh: fem: 8 (over z, y), basis: 4 (over x, core).
Axes of the slice: x: 2, y: 2, z: 4, core: 2. Of those that a mesh axis runs over, the one named last changes fastest.
Arguments:
- newest: float32 [128, 32768], P('basis', 'fem'), may hold values from -6 to 6
- earlier: float32 [16, 128, 32768], P('basis', None, 'fem'), may hold values from -0.03125 to 0.03125
- tiles: bfloat16 [256, 4, 128, 128], P('fem'), may hold values from -0.25 to 0.25
- tile_cols: int32 [256, 4], P('fem'), may hold values from 0 to 255, as said below
Outputs:
- orthogonal: float32 [128, 32768], P('basis', 'fem')
- coefficients: float32 [16, 128, 128], P('basis')
The draws below stay inside these ranges and needn't reach their ends.
Inputs may be any that keep to these rules, and one draw needn't show every extreme that they name: `tile_cols`: slot 0 of tile row t names t itself; every tile row of the rows of fem index p names only tiles from p * 32 - 2 to (p + 1) * 32 + 1; tiles may repeat in a row.
All inputs are finite; a program needn't handle non-finite values.
Results may differ from the reference program's by a relative error of at most 0.0029.
Values may be sent and summed in bfloat16 or wider, within the bound.
No kernel may reach another device: no remote copies, remote signals or barrier semaphores. Data moves between devices by JAX's collectives and lax.ppermute only.
A program may use at most 64 MiB of HBM per device.

```python
import jax
import jax.numpy as jnp
from jax import lax

BW = 128
TILE = 128
BLOCKS = 16
KT = 4
HALO_TILES = 2
RB = 32
NTB = 256
NROWS = 32768


def draw_tile_cols(key, part):
    row_ids = jnp.arange(NTB, dtype=jnp.int32)
    offsets = jax.random.randint(key, (NTB, KT), -HALO_TILES, RB + HALO_TILES, dtype=jnp.int32)
    anchor = row_ids // RB * RB
    columns = jnp.clip(anchor[:, None] + offsets, 0, NTB - 1)
    slot_ids = jnp.arange(KT, dtype=jnp.int32)[None, :]
    return jnp.where(slot_ids == 0, row_ids[:, None], columns).astype(jnp.int32)


def shard_levels(stream_key, extent, cuts, least, largest):
    factor_of = 1.0
    for axis_at, blocks in cuts:
        draws = jax.random.uniform(jax.random.fold_in(jax.random.fold_in(stream_key, 6), axis_at), (blocks,), jnp.float32, least / len(cuts), largest / len(cuts))
        factor_of = factor_of * jnp.repeat(jnp.exp(draws), extent[axis_at] // blocks).reshape((-1,) + (1,) * (len(extent) - 1 - axis_at))
    return factor_of


def centred(own_key, shape, width, most, cuts=(), kind=jnp.bfloat16):
    gain = shard_levels(own_key, shape, cuts, -0.22, 0.18) if cuts else 1.0
    array = jax.random.normal(own_key, shape, jnp.float32) * width * gain
    return jnp.minimum(jnp.maximum(array, -most), most).astype(kind)


def setup_inputs(seed: int = 0) -> dict:
    key_list = jax.random.split(jax.random.key(seed), 5)
    newest = centred(key_list[0], (BW, NROWS), 1.0, 6.0, ((0, 4), (1, 8)), jnp.float32)
    earlier = centred(key_list[1], (BLOCKS, BW, NROWS), NROWS ** -0.5, 0.03125, ((0, 4), (2, 8)), jnp.float32)
    tiles = centred(key_list[2], (NTB, KT, TILE, TILE), (KT * TILE) ** -0.5, 0.25, ((0, 8),))
    tile_cols = draw_tile_cols(jax.random.fold_in(key_list[4], 71), 0)
    return dict(newest=newest, earlier=earlier, tiles=tiles, tile_cols=tile_cols)


def project_out(current, earlier_rows):
    highest = lax.Precision.HIGHEST
    gram_block = lax.dot_general(earlier_rows, current, (((1,), (1,)), ((), ())), precision=highest, preferred_element_type=jnp.float32)
    removed = lax.dot_general(gram_block, earlier_rows, (((0,), (0,)), ((), ())), precision=highest, preferred_element_type=jnp.float32)
    return current - removed, gram_block


def reference(newest, earlier, tiles, tile_cols):
    highest = lax.Precision.HIGHEST
    rounded = lax.optimization_barrier(newest.astype(jnp.bfloat16)).astype(jnp.float32)
    tile_view = rounded.reshape(BW, NTB, TILE)
    picked = tile_view[:, tile_cols, :]
    image = jnp.einsum("ctkj,tkij->cti", picked, tiles.astype(jnp.float32), precision=highest)
    image = image.reshape(BW, NROWS)
    earlier_rows = earlier.reshape(BLOCKS * BW, NROWS)
    once, first = project_out(image, earlier_rows)
    twice, second = project_out(once, earlier_rows)
    return twice, (first + second).reshape(BLOCKS, BW, BW)
```

```python
import jax
import jax.numpy as jnp
from jax import lax
from jax.experimental import pallas as pl
from jax.experimental.pallas import tpu as pltpu
from jax.sharding import Mesh
from jax.sharding import PartitionSpec as P

HALO_TILES = 2
BF16 = jnp.bfloat16
F32 = jnp.float32
GROUP = ("fem", "core")
VMEM_LIMIT = 16 * 1024 * 1024


def shape(dims, dtype):
    return jax.ShapeDtypeStruct(dims, dtype)


WHOLE = pl.BlockSpec(memory_space=pltpu.VMEM)
AT = pl.BlockSpec(memory_space=pltpu.SMEM)


def call(body, name, arrays, ins, outs, out_shapes, scratch, flops, moved):
    return pl.pallas_call(
        body,
        out_shape=out_shapes,
        in_specs=ins,
        out_specs=outs,
        scratch_shapes=scratch,
        compiler_params=pltpu.CompilerParams(vmem_limit_bytes=VMEM_LIMIT),
        cost_estimate=pl.CostEstimate(flops=flops, bytes_accessed=moved, transcendentals=0),
        name=name,
    )(*arrays)


def dot_nt(a, b):
    return lax.dot_general(a, b, (((1,), (1,)), ((), ())), preferred_element_type=F32)


def dot_nn(a, b):
    return lax.dot_general(a, b, (((1,), (0,)), ((), ())), preferred_element_type=F32)


def halve(place, earlier):
    blocks, width, length = earlier.shape
    half = length // 2

    def body(place, earlier, keep, send):
        for start, out in ((1 - place[1], send), (place[1], keep)):
            columns = pl.ds(pl.multiple_of(start * half, half), half)
            for b in range(blocks):
                out[b * width : (b + 1) * width, :] = earlier[b, :, columns].astype(BF16)

    return call(
        body, "halve", (place, earlier),
        [AT, WHOLE],
        [WHOLE] * 2,
        [shape((blocks * width, half), BF16)] * 2,
        [], 0, 6 * blocks * width * length,
    )


def apply_operator(place, cols, newest, before, after, tiles):
    count, length = newest.shape
    tile_rows, slots, tile, _ = tiles.shape
    half, steps = length // 2, 2
    per = tile_rows // (2 * steps)

    def body(place, cols, newest, before, after, tiles, other, own, other16, own16, grid):
        for m in range(HALO_TILES):
            grid[m] = before[:, m * tile : (m + 1) * tile]
            grid[HALO_TILES + tile_rows + m] = after[:, m * tile : (m + 1) * tile]
        for m in range(tile_rows):
            grid[HALO_TILES + m] = newest[:, m * tile : (m + 1) * tile].astype(BF16)
        shift = HALO_TILES - place[2] * tile_rows
        for side, out, out16 in ((1 - place[1], other, other16), (place[1], own, own16)):

            def step(i, _):
                first = (side * steps + i) * per
                for r in range(per):
                    picked = [grid[cols[k, first + r] + shift] for k in range(slots)]
                    stored = [tiles[first + r, k] for k in range(slots)]
                    value = dot_nt(jnp.concatenate(picked, axis=1), jnp.concatenate(stored, axis=1))
                    at = pl.ds(pl.multiple_of((i * per + r) * tile, tile), tile)
                    out[:, at] = value
                    out16[:, at] = value.astype(BF16)

            lax.fori_loop(0, steps, step, None)

    return call(
        body, "image", (place, cols, newest, before, after, tiles),
        [AT, AT] + [WHOLE] * 4,
        [WHOLE] * 4,
        [shape((count, half), F32)] * 2 + [shape((count, half), BF16)] * 2,
        [pltpu.VMEM((tile_rows + 2 * HALO_TILES, count, tile), BF16)],
        2 * count * length * slots * tile,
        2 * tiles.size,
    )


def inner_first(place, keep, recv, same, cross):
    count, half = keep.shape
    cols = same.shape[0]

    def body(place, keep, recv, same, cross, out, w):
        w[place[1]] = same[...].astype(BF16)
        w[1 - place[1]] = cross[...].astype(BF16)
        full = w[...].reshape(2 * cols, half)
        kept, got = dot_nt(keep[...], full), dot_nt(recv[...], full)
        low = place[1] == 0
        out[...] = jnp.concatenate([jnp.where(low, kept, got), jnp.where(low, got, kept)], axis=1).astype(BF16)

    return call(
        body, "inner_first", (place, keep, recv, same, cross),
        [AT] + [WHOLE] * 4,
        WHOLE,
        shape((count, 4 * cols), BF16),
        [pltpu.VMEM((2, cols, half), BF16)],
        8 * count * half * cols,
        4 * keep.size,
    )


def inner_second(place, keep, recv, rest, message):
    count, half = keep.shape
    cols = 2 * rest.shape[1]

    def body(place, keep, recv, rest, message, out, once):
        value = rest[...].reshape(cols, half) - message[...].reshape(cols, half).astype(F32)
        high = value.astype(BF16)
        once[:cols] = high
        once[cols:] = (value - high.astype(F32)).astype(BF16)
        kept, got = dot_nt(keep[...], once[...]), dot_nt(recv[...], once[...])
        kept, got = kept[:, :cols] + kept[:, cols:], got[:, :cols] + got[:, cols:]
        low = place[1] == 0
        out[...] = jnp.concatenate([jnp.where(low, kept, got), jnp.where(low, got, kept)], axis=1)

    return call(
        body, "inner_second", (place, keep, recv, rest, message),
        [AT] + [WHOLE] * 4,
        WHOLE,
        shape((count, 2 * cols), F32),
        [pltpu.VMEM((2 * cols, half), BF16)],
        8 * count * half * cols,
        4 * keep.size,
    )


def turned_rows(place, packed, turned):
    turned[...] = packed.T.astype(BF16).reshape(turned.shape)
    return turned[place[1]], turned[1 - place[1]]


def expand_first(place, first, keep, recv, same, cross, exact):
    count, half = keep.shape
    cols = same.shape[0]
    per = half // 4

    def body(place, first, keep, recv, same, cross, rest, message, turned, u):
        kept, got = turned_rows(place, first[...].astype(F32), turned)
        for i in range(half // per):
            part = slice(i * per, (i + 1) * per)
            u[...] = (dot_nn(kept, keep[:, part]) + dot_nn(got, recv[:, part])).reshape(2, cols, per)
            for at, piece in ((place[1], same), (1 - place[1], cross)):
                value = piece[:, part].astype(F32)
                rest[at, :, part] = value - u[at]
                low = value - value.astype(BF16).astype(F32) if exact else 0.0
                message[at, :, part] = (u[at] - low).astype(BF16)

    return call(
        body, "expand_first", (place, first, keep, recv, same, cross),
        [AT] + [WHOLE] * 5,
        [WHOLE] * 2,
        [shape((2, cols, half), F32), shape((2, cols, half), BF16)],
        [pltpu.VMEM((2, 2 * cols, count), BF16), pltpu.VMEM((2, cols, per), F32)],
        8 * count * half * cols,
        4 * keep.size,
    )


def expand_total(place, first, second, keep, recv):
    count, half = keep.shape
    cols = first.shape[1] // 4
    per = half // 4

    def body(place, first, second, keep, recv, same, cross, turned, u):
        kept, got = turned_rows(place, first[...].astype(F32) + second[...].astype(F32), turned)
        for i in range(half // per):
            part = slice(i * per, (i + 1) * per)
            u[...] = (dot_nn(kept, keep[:, part]) + dot_nn(got, recv[:, part])).reshape(2, cols, per)
            same[:, part] = u[place[1]].astype(BF16)
            cross[:, part] = u[1 - place[1]].astype(BF16)

    return call(
        body, "expand_total", (place, first, second, keep, recv),
        [AT] + [WHOLE] * 4,
        [WHOLE] * 2,
        [shape((cols, half), BF16)] * 2,
        [pltpu.VMEM((2, 2 * cols, count), BF16), pltpu.VMEM((2, cols, per), F32)],
        8 * count * half * cols,
        4 * keep.size,
    )


def coefficients(place, parts):
    count, lanes = parts[0].shape
    cols = lanes // 2

    def body(place, first_a, second_a, first_b, second_b, out):
        def own(first, second):
            total = first[...].astype(F32) + second[...].astype(F32)
            return jnp.where(place[1] == 0, total[:, :cols], total[:, cols:])

        a, b = own(first_a, second_a), own(first_b, second_b)
        low = place[0] == 0
        out[...] = jnp.concatenate([jnp.where(low, a, b), jnp.where(low, b, a)], axis=1)

    return call(
        body, "coefficients", (place, *parts),
        [AT] + [WHOLE] * 4,
        WHOLE,
        shape((count, lanes), F32),
        [], 0, 12 * count * lanes,
    )


def subtract(place, own, other, mine, peer, same, diagonal):
    cols, half = own.shape

    def body(place, own, other, mine, peer, same, diagonal, out):
        out[:, pl.ds(pl.multiple_of(place[1] * half, half), half)] = own[...] - (
            mine[...].astype(F32) + same[...].astype(F32)
        )
        out[:, pl.ds(pl.multiple_of((1 - place[1]) * half, half), half)] = other[...] - (
            peer[...].astype(F32) + diagonal[...].astype(F32)
        )

    return call(
        body, "subtract", (place, own, other, mine, peer, same, diagonal),
        [AT] + [WHOLE] * 6,
        WHOLE,
        shape((cols, 2 * half), F32),
        [], 0, 20 * cols * half,
    )


def swap(value, axes):
    if axes == ("x", "core"):
        return lax.ppermute(value, axes, [(i, 3 - i) for i in range(4)])
    return lax.ppermute(value, axes[0], [(0, 1), (1, 0)])


def sum_over_group(partial):
    group = lax.axis_size("fem") * 2
    chunks = partial.reshape(group, -1, partial.shape[-1])
    chunks = lax.all_to_all(chunks, GROUP, 0, 0, tiled=True)
    return jnp.sum(chunks.astype(F32), axis=0).astype(BF16)


def spread(chunk):
    group = lax.axis_size("fem") * 2
    copies = jnp.broadcast_to(chunk[None], (group,) + chunk.shape)
    return lax.all_to_all(copies, GROUP, 0, 0, tiled=True).reshape(-1, chunk.shape[1])


def shards(newest, earlier, tiles, tile_cols):
    blocks, width, length = earlier.shape
    edge = HALO_TILES * tiles.shape[2]
    place = jnp.stack([lax.axis_index(name) for name in ("x", "core", "fem")]).astype(jnp.int32)
    devices = lax.axis_size("fem")
    up = [(i, i + 1) for i in range(devices - 1)]
    last, start = lax.optimization_barrier((newest[:, length - edge :], newest[:, :edge]))
    before = lax.ppermute(last.astype(BF16), "fem", up)
    after = lax.ppermute(start.astype(BF16), "fem", [(j, i) for i, j in up])
    keep, send = halve(place, earlier)
    send, before, after = lax.optimization_barrier((send, before, after))
    recv = swap(send, ("core",))
    other, own, other16, own16 = apply_operator(place, tile_cols.T, newest, before, after, tiles)
    peer = swap(other, ("core",))
    diagonal = swap(other16, ("x", "core"))
    same = swap(own16, ("x",))
    first_a = spread(sum_over_group(inner_first(place, keep, recv, own16, peer)))
    first_b = spread(sum_over_group(inner_first(place, keep, recv, same, diagonal)))
    rest_a, message_a = expand_first(place, first_a, keep, recv, own, peer, True)
    rest_b, message_b = expand_first(place, first_b, keep, recv, same, diagonal, False)
    message_a, message_b = swap(message_b, ("x",)), swap(message_a, ("x",))
    second_b = spread(sum_over_group(inner_second(place, keep, recv, rest_b, message_b)))
    second_a = spread(sum_over_group(inner_second(place, keep, recv, rest_a, message_a)))
    same, diagonal = expand_total(place, first_b, second_b, keep, recv)
    diagonal = swap(diagonal, ("x", "core"))
    same = swap(same, ("x",))
    mine, peer = expand_total(place, first_a, second_a, keep, recv)
    peer = swap(peer, ("core",))
    coeffs = coefficients(place, (first_a, second_a, first_b, second_b))
    return subtract(place, own, other, mine, peer, same, diagonal), coeffs.reshape(blocks, width, -1)


def solution(mesh):
    devices = mesh.devices
    split = Mesh(devices.reshape(devices.shape[0], 2, 2), ("fem", "x", "core"))
    basis = ("x", "core")
    placed = (
        P(basis, "fem"),
        P(basis, None, "fem"),
        P("fem", None, None, None),
        P("fem", None),
    )
    return jax.shard_map(
        shards,
        mesh=split,
        in_specs=placed,
        out_specs=(P(basis, "fem"), P(basis, None, None)),
        check_vma=False,
    )
```
